32 devices in a mesh: seq: 16 (over z, y, core), dp: 2 (over x).
Axes of the slice: x: 2, y: 2, z: 4, core: 2. Of those that a mesh axis runs over, the one named last changes fastest.
Arguments:
- tokens: bfloat16 [2, 4096, 4096], P('dp', 'seq'), may hold values from -6 to 6
- query: bfloat16 [2, 4096, 2048], P('dp', 'seq'), may hold values from -5 to 5
- key: bfloat16 [2, 4096, 2048], P('dp', 'seq'), may hold values from -5 to 5
- value: bfloat16 [2, 4096, 2048], P('dp', 'seq'), may hold values from -6 to 6
- output_gradient: bfloat16 [2, 4096, 2048], P('dp', 'seq'), may hold values from -24 to 24
- adapter_down_weight: bfloat16 [3, 8, 4096], replicated, may hold values from -0.09375 to 0.09375
- adapter_up_weight: bfloat16 [3, 8, 2048], replicated, may hold values from -2 to 2
Outputs:
- grad_query: bfloat16 [2, 4096, 2048], P('dp', 'seq')
- grad_key: bfloat16 [2, 4096, 2048], P('dp', 'seq')
- grad_value: bfloat16 [2, 4096, 2048], P('dp', 'seq')
- grad_down: float32 [3, 8, 4096], replicated
- grad_up: float32 [3, 8, 2048], replicated
The draws below stay inside these ranges and needn't reach their ends.
All inputs are finite; a program needn't handle non-finite values.
Results may differ from the reference program's by a relative error of at most 0.011.
Values may be sent and summed in bfloat16 or wider, within the bound.
A program may use at most 64 MiB of HBM per device.

```python
import math
import jax
import jax.numpy as jnp
from jax import lax

MODEL_WIDTH = 4096
SHIFTED_HEADS = 16
HEAD_FEATURES = 128
ADAPTER_RANK = 8
TOK_DEV = 256
SHIFT = 128
SEQUENCE_LENGTH = 4096
BATCH_COUNT = 2
N_SEQ = 16


def draw_query(key, part):
    key = jax.random.fold_in(key, 31)
    shape = (BATCH_COUNT, SEQUENCE_LENGTH, SHIFTED_HEADS * HEAD_FEATURES)
    return jnp.clip(jax.random.normal(key, shape), -4.5, 4.5).astype(jnp.bfloat16)


def draw_key(key, part):
    key = jax.random.fold_in(key, 32)
    shape = (BATCH_COUNT, SEQUENCE_LENGTH, SHIFTED_HEADS * HEAD_FEATURES)
    return jnp.clip(jax.random.normal(key, shape), -4.5, 4.5).astype(jnp.bfloat16)


def steps_of(key, dims, pieces, least, top_value):
    level = 1.0
    for axis_at, parts in pieces:
        heights = jax.random.uniform(jax.random.fold_in(jax.random.fold_in(key, 6), axis_at), (parts,), jnp.float32, least / len(pieces), top_value / len(pieces))
        level = level * jnp.repeat(jnp.exp(heights), dims[axis_at] // parts).reshape((-1,) + (1,) * (len(dims) - 1 - axis_at))
    return level


def normal_values(key, extent, scale, most, pieces=(), dtype=jnp.bfloat16):
    values = jax.random.normal(key, extent, jnp.float32) * scale
    if len(pieces) > 0:
        values = steps_of(key, extent, pieces, -0.22, 0.18) * values
    return jnp.clip(values, min=-most, max=most).astype(dtype)


def setup_inputs(seed: int = 0) -> dict:
    streams_of = jax.random.split(jax.random.key(seed), 8)
    return {
        "tokens": normal_values(streams_of[0], (BATCH_COUNT, SEQUENCE_LENGTH, MODEL_WIDTH), 1.0, 6.0, ((0, 2), (1, 16))),
        "query": draw_query(jax.random.fold_in(streams_of[7], 71), 0),
        "key": draw_key(jax.random.fold_in(streams_of[7], 71), 0),
        "value": normal_values(streams_of[3], (BATCH_COUNT, SEQUENCE_LENGTH, SHIFTED_HEADS * HEAD_FEATURES), 1.0, 6.0, ((0, 2), (1, 16))),
        "output_gradient": normal_values(streams_of[4], (BATCH_COUNT, SEQUENCE_LENGTH, SHIFTED_HEADS * HEAD_FEATURES), 4.0, 24.0, ((0, 2), (1, 16))),
        "adapter_down_weight": normal_values(streams_of[5], (3, ADAPTER_RANK, MODEL_WIDTH), MODEL_WIDTH ** -0.5, 0.09375),
        "adapter_up_weight": normal_values(streams_of[6], (3, ADAPTER_RANK, SHIFTED_HEADS * HEAD_FEATURES), ADAPTER_RANK ** -0.5, 2.0),
    }


adapter_scale = 2.0

def group_back(query, key, value, output_gradient):
    rows = query.shape[0]
    scale_factor = 1.0 / math.sqrt(HEAD_FEATURES)
    qf = query.astype(jnp.float32)
    kf = key.astype(jnp.float32)
    vf = value.astype(jnp.float32)
    gf = output_gradient.astype(jnp.float32)
    scores = jnp.einsum('qhd,khd->hqk', qf, kf) * scale_factor
    causal = jnp.arange(rows)[:, None] >= jnp.arange(rows)[None, :]
    scores = jnp.where(causal[None], scores, -jnp.inf)
    highest = lax.optimization_barrier(jnp.max(scores, axis=-1, keepdims=True))
    raised = jnp.exp(scores - highest)
    weights = raised / lax.optimization_barrier(jnp.sum(raised, axis=-1, keepdims=True))
    weights_low = lax.optimization_barrier(weights.astype(jnp.bfloat16)).astype(jnp.float32)
    attended = jnp.einsum('hqk,khd->qhd', weights_low, vf)
    row_dots = lax.optimization_barrier(jnp.sum(gf * attended, axis=-1))
    grad_value = jnp.einsum('hqk,qhd->khd', weights_low, gf)
    grad_weights = jnp.einsum('qhd,khd->hqk', gf, vf)
    grad_scores = weights * (grad_weights - row_dots.T[:, :, None])
    grad_scores = lax.optimization_barrier(grad_scores.astype(jnp.bfloat16)).astype(jnp.float32)
    grad_query = jnp.einsum('hqk,khd->qhd', grad_scores, kf) * scale_factor
    grad_key = jnp.einsum('hqk,qhd->khd', grad_scores, qf) * scale_factor
    return (grad_query.astype(jnp.bfloat16), grad_key.astype(jnp.bfloat16), grad_value.astype(jnp.bfloat16))

def reference(tokens, query, key, value, output_gradient, adapter_down_weight, adapter_up_weight):
    half_heads = SHIFTED_HEADS // 2

    def arrange(array):
        heads = array.reshape(BATCH_COUNT, SEQUENCE_LENGTH, SHIFTED_HEADS, HEAD_FEATURES)
        moved = jnp.roll(heads[:, :, half_heads:], -SHIFT, axis=1)
        joined = jnp.concatenate([heads[:, :, :half_heads], moved], axis=2)
        return joined.reshape(BATCH_COUNT * N_SEQ, TOK_DEV, SHIFTED_HEADS, HEAD_FEATURES)

    def restore(array):
        heads = array.reshape(BATCH_COUNT, SEQUENCE_LENGTH, SHIFTED_HEADS, HEAD_FEATURES)
        moved = jnp.roll(heads[:, :, half_heads:], SHIFT, axis=1)
        joined = jnp.concatenate([heads[:, :, :half_heads], moved], axis=2)
        return joined.reshape(BATCH_COUNT, SEQUENCE_LENGTH, SHIFTED_HEADS * HEAD_FEATURES)
    grouped = (arrange(query), arrange(key), arrange(value), arrange(output_gradient))
    results = lax.map(lambda items: group_back(items[0], items[1], items[2], items[3]), grouped)
    grads = [restore(results[0]), restore(results[1]), restore(results[2])]
    flattened_tokens = tokens.reshape(BATCH_COUNT * SEQUENCE_LENGTH, MODEL_WIDTH)
    scale_factor = adapter_scale / math.sqrt(BATCH_COUNT * SEQUENCE_LENGTH)
    downs = []
    ups = []
    for projection_index in range(3):
        flattened_gradient = grads[projection_index].reshape(BATCH_COUNT * SEQUENCE_LENGTH, SHIFTED_HEADS * HEAD_FEATURES)
        down_projected = jnp.dot(flattened_tokens, adapter_down_weight[projection_index].T, preferred_element_type=jnp.float32).astype(jnp.bfloat16)
        returned_values = jnp.dot(flattened_gradient, adapter_up_weight[projection_index].T, preferred_element_type=jnp.float32).astype(jnp.bfloat16)
        downs.append(jnp.dot(returned_values.T, flattened_tokens, preferred_element_type=jnp.float32) * scale_factor)
        ups.append(jnp.dot(down_projected.T, flattened_gradient, preferred_element_type=jnp.float32) * scale_factor)
    return (grads[0], grads[1], grads[2], jnp.stack(downs), jnp.stack(ups))
```

```python
import functools
import math

import jax
import jax.numpy as jnp
from jax import lax
from jax.experimental import pallas as pl
from jax.experimental.pallas import tpu as pltpu
from jax.sharding import PartitionSpec as P

HEAD_FEATURES = 128
ADAPTER_SCALE = 2.0
PLANE_SEQ = 4
F32 = jnp.float32
BF16 = jnp.bfloat16
MESH = pl.DeviceIdType.MESH


def dot(a, b, dims):
    return lax.dot_general(a, b, (dims, ((), ())), preferred_element_type=F32)


def attend_back(query, key, value, gradient, offset):
    scale = 1.0 / math.sqrt(HEAD_FEATURES)
    scores = dot(key, query, ((1,), (1,)))
    shape = scores.shape
    keep = lax.broadcasted_iota(jnp.int32, shape, 0) <= (
        lax.broadcasted_iota(jnp.int32, shape, 1) + offset
    )
    scores = jnp.where(keep, scores, -jnp.inf)
    highest = jnp.max(scores, axis=0, keepdims=True)
    raised = jnp.exp2((scores - highest) * (scale * math.log2(math.e)))
    weights = raised * (1.0 / jnp.sum(raised, axis=0, keepdims=True))
    weights_low = weights.astype(BF16)
    grad_weights = dot(value, gradient, ((1,), (1,)))
    row_dots = jnp.sum(weights_low.astype(F32) * grad_weights, axis=0, keepdims=True)
    grad_scores = (weights * (grad_weights - row_dots)).astype(BF16)
    grad_value = dot(weights_low, gradient, ((1,), (0,)))
    grad_key = dot(grad_scores, query, ((1,), (0,))) * scale
    grad_query = dot(grad_scores, key, ((0,), (0,))) * scale
    return grad_query, grad_key, grad_value


def kernel(
    n_seq, n_dp, tok, q, k, v, g, down_w, up_w, gq, gk, gv, gd, gu,
    kv_in, ret_out, ret_in, part, rs_out, rs_in, zbuf, gbuf,
    kv_send, kv_recv, ret_send, ret_recv, rs_send, rs_recv, z_send, z_recv, ag_send, ag_recv,
):
    rows, width = q.shape[1:]
    model_width = tok.shape[2]
    half, half_width = rows // 2, width // 2
    heads = half_width // HEAD_FEATURES
    seq, dp = lax.axis_index("seq"), lax.axis_index("dp")
    right, left = lax.rem(seq + 1, n_seq), lax.rem(seq + n_seq - 1, n_seq)
    n_plane, n_z = n_dp * PLANE_SEQ, n_seq // PLANE_SEQ
    mine, zone = dp * PLANE_SEQ + lax.rem(seq, PLANE_SEQ), seq // PLANE_SEQ

    def plane_id(j):
        c = lax.rem(mine + j, n_plane)
        return c, {"seq": zone * PLANE_SEQ + lax.rem(c, PLANE_SEQ), "dp": c // PLANE_SEQ}

    def zone_id(j):
        z = lax.rem(zone + j, n_z)
        return z, {"seq": z * PLANE_SEQ + lax.rem(seq, PLANE_SEQ), "dp": dp}

    def remote(src, dst, send, recv, target):
        return pltpu.make_async_remote_copy(
            src_ref=src, dst_ref=dst, send_sem=send, recv_sem=recv,
            device_id=target, device_id_type=MESH,
        )

    barrier = pltpu.get_barrier_semaphore()
    targets = [{"seq": left, "dp": dp}, {"seq": right, "dp": dp}]
    targets += [plane_id(j)[1] for j in range(1, n_plane)]
    targets += [zone_id(j)[1] for j in range(1, n_z)]
    for target in targets:
        pl.semaphore_signal(barrier, inc=1, device_id=target, device_id_type=MESH)
    pl.semaphore_wait(barrier, len(targets))

    upper, lower = pl.ds(half, half), pl.ds(0, half)
    shifted = pl.ds(half_width, half_width)
    kv_copies = [
        remote(
            ref.at[0, upper, shifted], kv_in.at[i], kv_send.at[i], kv_recv.at[i],
            {"seq": right, "dp": dp},
        )
        for i, ref in enumerate((k, v))
    ]
    for copy in kv_copies:
        copy.start()

    def cols(h):
        return pl.ds(pl.multiple_of(h * HEAD_FEATURES, HEAD_FEATURES), HEAD_FEATURES)

    @pl.loop(0, heads, unroll=2)
    def _(h):
        c = cols(h)
        dq, dk, dv = attend_back(q[0, :, c], k[0, :, c], v[0, :, c], g[0, :, c], 0)
        gq[0, :, c] = dq.astype(BF16)
        gk[0, :, c] = dk.astype(BF16)
        gv[0, :, c] = dv.astype(BF16)

    @pl.loop(0, heads, unroll=4)
    def _(h):
        c, s = cols(h + heads), cols(h)
        dq, dk, dv = attend_back(
            q[0, upper, c], k[0, upper, c], v[0, upper, c], g[0, upper, c], 0
        )
        gq[0, upper, c] = dq.astype(BF16)
        part[0, :, s] = dk
        part[1, :, s] = dv

    for copy in kv_copies:
        copy.wait_recv()
    ret_copies = []
    chunks = ret_send.shape[0] // 2
    per = heads // chunks
    for chunk in range(chunks):
        @pl.loop(chunk * per, (chunk + 1) * per, unroll=2)
        def _(h):
            c, s = cols(h + heads), cols(h)
            keys = jnp.concatenate([kv_in[0, :, s], k[0, lower, c]], axis=0)
            values = jnp.concatenate([kv_in[1, :, s], v[0, lower, c]], axis=0)
            dq, dk, dv = attend_back(q[0, lower, c], keys, values, g[0, lower, c], half)
            gq[0, lower, c] = dq.astype(BF16)
            gk[0, lower, c] = dk[half:].astype(BF16)
            gv[0, lower, c] = dv[half:].astype(BF16)
            ret_out[0, :, s] = dk[:half].astype(BF16)
            ret_out[1, :, s] = dv[:half].astype(BF16)

        span = pl.ds(chunk * per * HEAD_FEATURES, per * HEAD_FEATURES)
        for i in range(2):
            at = chunk * 2 + i
            copy = remote(
                ret_out.at[i, :, span], ret_in.at[i, :, span], ret_send.at[at], ret_recv.at[at],
                {"seq": left, "dp": dp},
            )
            copy.start()
            ret_copies.append(copy)

    down_all = jnp.concatenate([down_w[p].astype(F32) for p in range(3)], axis=0).astype(BF16)
    projected = dot(down_all, tok[0], ((1,), (1,)))
    ranks = down_w.shape[1]
    returned, ups = [], []
    for p, ref in enumerate((gq, gk, gv)):
        if p == 1:
            for copy in ret_copies:
                copy.wait_recv()
            gk[0, upper, shifted] = (part[0] + ret_in[0].astype(F32)).astype(BF16)
            gv[0, upper, shifted] = (part[1] + ret_in[1].astype(F32)).astype(BF16)
        grad = ref[0]
        returned.append(dot(up_w[p], grad, ((1,), (1,))))
        ups.append(dot(projected[p * ranks:(p + 1) * ranks].astype(BF16), grad, ((1,), (0,))))
    downs = dot(jnp.concatenate(returned, axis=0).astype(BF16), tok[0], ((1,), (0,)))
    ups = jnp.concatenate(ups, axis=0)

    wd, wu = model_width // n_plane, width // n_plane
    wide = (wd + wu) // 2
    for c in range(n_plane):
        rs_out[c] = jnp.concatenate(
            [
                downs[:, c * wd:c * wd + wide],
                jnp.concatenate(
                    [downs[:, c * wd + wide:(c + 1) * wd], ups[:, c * wu:(c + 1) * wu]], axis=1
                ),
            ],
            axis=0,
        ).astype(BF16)
    copies = []
    for j in range(1, n_plane):
        c, target = plane_id(j)
        copy = remote(rs_out.at[c], rs_in.at[mine], rs_send.at[j], rs_recv.at[j], target)
        copy.start()
        copies.append(copy)
    total = rs_out[mine].astype(F32)
    for j in range(1, n_plane):
        c = lax.rem(mine + n_plane - j, n_plane)
        remote(rs_out.at[c], rs_in.at[c], rs_send.at[j], rs_recv.at[j], plane_id(j)[1]).wait_recv()
        total = total + rs_in[c].astype(F32)
    zbuf[zone] = total.astype(BF16)
    for j in range(1, n_z):
        _, target = zone_id(j)
        copy = remote(zbuf.at[zone], zbuf.at[zone], z_send.at[j], z_recv.at[j], target)
        copy.start()
        copies.append(copy)
    for j in range(1, n_z):
        z = lax.rem(zone + n_z - j, n_z)
        remote(zbuf.at[z], zbuf.at[z], z_send.at[j], z_recv.at[j], zone_id(j)[1]).wait_recv()
    total = zbuf[0].astype(F32)
    for z in range(1, n_z):
        total = total + zbuf[z].astype(F32)
    factor = ADAPTER_SCALE / math.sqrt(rows * n_seq * n_dp)
    gbuf[mine] = (total * factor).astype(BF16)
    for j in range(1, n_plane):
        _, target = plane_id(j)
        copy = remote(gbuf.at[mine], gbuf.at[mine], ag_send.at[j], ag_recv.at[j], target)
        copy.start()
        copies.append(copy)
    for j in range(1, n_plane):
        c = lax.rem(mine + n_plane - j, n_plane)
        remote(gbuf.at[c], gbuf.at[c], ag_send.at[j], ag_recv.at[j], plane_id(j)[1]).wait_recv()
    for c in range(n_plane):
        both = gbuf[c].astype(F32)
        n = both.shape[0] // 2
        down = jnp.concatenate([both[:n], both[n:, :wd - wide]], axis=1)
        up = both[n:, wd - wide:]
        for p in range(3):
            gd[p, :, c * wd:(c + 1) * wd] = down[p * ranks:(p + 1) * ranks]
            gu[p, :, c * wu:(c + 1) * wu] = up[p * ranks:(p + 1) * ranks]
    for copy in kv_copies + ret_copies + copies:
        copy.wait_send()


def shards(n_seq, n_dp, tokens, query, key, value, gradient, down_w, up_w):
    _, rows, width = query.shape
    half, half_width = rows // 2, width // 2
    projections, ranks, model_width = down_w.shape
    n_plane, n_z = n_dp * PLANE_SEQ, n_seq // PLANE_SEQ
    piece = (2 * projections * ranks, (model_width + width) // n_plane // 2)
    dma = pltpu.SemaphoreType.DMA
    vmem = pl.BlockSpec(memory_space=pltpu.VMEM)
    return pl.pallas_call(
        functools.partial(kernel, n_seq, n_dp),
        out_shape=[jax.ShapeDtypeStruct(query.shape, BF16)] * 3
        + [jax.ShapeDtypeStruct(down_w.shape, F32), jax.ShapeDtypeStruct(up_w.shape, F32)],
        in_specs=[vmem] * 7,
        out_specs=[vmem] * 5,
        scratch_shapes=[
            pltpu.VMEM((2, half, half_width), BF16),
            pltpu.VMEM((2, half, half_width), BF16),
            pltpu.VMEM((2, half, half_width), BF16),
            pltpu.VMEM((2, half, half_width), F32),
            pltpu.VMEM((n_plane,) + piece, BF16),
            pltpu.VMEM((n_plane,) + piece, BF16),
            pltpu.VMEM((n_z,) + piece, BF16),
            pltpu.VMEM((n_plane,) + piece, BF16),
            dma((2,)), dma((2,)), dma((4,)), dma((4,)),
            dma((n_plane,)), dma((n_plane,)), dma((n_z,)), dma((n_z,)),
            dma((n_plane,)), dma((n_plane,)),
        ],
        compiler_params=pltpu.CompilerParams(
            collective_id=0, has_side_effects=True, vmem_limit_bytes=56 * 1024 * 1024
        ),
    )(tokens, query, key, value, gradient, down_w, up_w)


def solution(mesh):
    split = P("dp", "seq", None)
    return jax.shard_map(
        functools.partial(shards, mesh.shape["seq"], mesh.shape["dp"]),
        mesh=mesh,
        in_specs=(split,) * 5 + (P(), P()),
        out_specs=(split,) * 3 + (P(), P()),
        check_vma=False,
    )
```

```python
import functools
import math

import jax
import jax.numpy as jnp
from jax import lax
from jax.experimental import pallas as pl
from jax.experimental.pallas import tpu as pltpu
from jax.sharding import PartitionSpec as P

HEAD_FEATURES = 128
ADAPTER_SCALE = 2.0
PLANE_SEQ = 4
F32 = jnp.float32
BF16 = jnp.bfloat16
MESH = pl.DeviceIdType.MESH


def dot(a, b, dims):
    return lax.dot_general(a, b, (dims, ((), ())), preferred_element_type=F32)


def attend_back(query, key, value, gradient, offset):
    scale = 1.0 / math.sqrt(HEAD_FEATURES)
    scores = dot(key, query, ((1,), (1,)))
    shape = scores.shape
    keep = lax.broadcasted_iota(jnp.int32, shape, 0) <= (
        lax.broadcasted_iota(jnp.int32, shape, 1) + offset
    )
    scores = jnp.where(keep, scores, -jnp.inf)
    highest = jnp.max(scores, axis=0, keepdims=True)
    raised = jnp.exp2((scores - highest) * (scale * math.log2(math.e)))
    weights = raised * (1.0 / jnp.sum(raised, axis=0, keepdims=True))
    weights_low = weights.astype(BF16)
    grad_weights = dot(value, gradient, ((1,), (1,)))
    row_dots = jnp.sum(weights_low.astype(F32) * grad_weights, axis=0, keepdims=True)
    grad_scores = (weights * (grad_weights - row_dots)).astype(BF16)
    grad_value = dot(weights_low, gradient, ((1,), (0,)))
    grad_key = dot(grad_scores, query, ((1,), (0,))) * scale
    grad_query = dot(grad_scores, key, ((0,), (0,))) * scale
    return grad_query, grad_key, grad_value


def kernel(
    n_seq, n_dp, tok, q, k, v, g, down_w, up_w, gq, gk, gv, gbuf_out,
    kv_in, ret_out, ret_in, part, rs_out, rs_in, zbuf, gbuf,
    kv_send, kv_recv, ret_send, ret_recv, rs_send, rs_recv, z_send, z_recv, ag_send, ag_recv,
):
    rows, width = q.shape[1:]
    model_width = tok.shape[2]
    half, half_width = rows // 2, width // 2
    heads = half_width // HEAD_FEATURES
    seq, dp = lax.axis_index("seq"), lax.axis_index("dp")
    right, left = lax.rem(seq + 1, n_seq), lax.rem(seq + n_seq - 1, n_seq)
    n_plane, n_z = n_dp * PLANE_SEQ, n_seq // PLANE_SEQ
    mine, zone = dp * PLANE_SEQ + lax.rem(seq, PLANE_SEQ), seq // PLANE_SEQ

    def plane_id(j):
        c = lax.rem(mine + j, n_plane)
        return c, {"seq": zone * PLANE_SEQ + lax.rem(c, PLANE_SEQ), "dp": c // PLANE_SEQ}

    def zone_id(j):
        z = lax.rem(zone + j, n_z)
        return z, {"seq": z * PLANE_SEQ + lax.rem(seq, PLANE_SEQ), "dp": dp}

    def remote(src, dst, send, recv, target):
        return pltpu.make_async_remote_copy(
            src_ref=src, dst_ref=dst, send_sem=send, recv_sem=recv,
            device_id=target, device_id_type=MESH,
        )

    barrier = pltpu.get_barrier_semaphore()
    targets = [{"seq": left, "dp": dp}, {"seq": right, "dp": dp}]
    targets += [plane_id(j)[1] for j in range(1, n_plane)]
    targets += [zone_id(j)[1] for j in range(1, n_z)]
    for target in targets:
        pl.semaphore_signal(barrier, inc=1, device_id=target, device_id_type=MESH)
    pl.semaphore_wait(barrier, len(targets))

    upper, lower = pl.ds(half, half), pl.ds(0, half)
    shifted = pl.ds(half_width, half_width)
    kv_copies = [
        remote(
            ref.at[0, upper, shifted], kv_in.at[i], kv_send.at[i], kv_recv.at[i],
            {"seq": right, "dp": dp},
        )
        for i, ref in enumerate((k, v))
    ]
    for copy in kv_copies:
        copy.start()

    def cols(h):
        return pl.ds(pl.multiple_of(h * HEAD_FEATURES, HEAD_FEATURES), HEAD_FEATURES)

    @pl.loop(0, heads, unroll=2)
    def _(h):
        c = cols(h)
        dq, dk, dv = attend_back(q[0, :, c], k[0, :, c], v[0, :, c], g[0, :, c], 0)
        gq[0, :, c] = dq.astype(BF16)
        gk[0, :, c] = dk.astype(BF16)
        gv[0, :, c] = dv.astype(BF16)

    @pl.loop(0, heads, unroll=4)
    def _(h):
        c, s = cols(h + heads), cols(h)
        dq, dk, dv = attend_back(
            q[0, upper, c], k[0, upper, c], v[0, upper, c], g[0, upper, c], 0
        )
        gq[0, upper, c] = dq.astype(BF16)
        part[0, :, s] = dk
        part[1, :, s] = dv

    for copy in kv_copies:
        copy.wait_recv()
    ret_copies = []
    chunks = ret_send.shape[0] // 2
    per = heads // chunks
    for chunk in range(chunks):
        @pl.loop(chunk * per, (chunk + 1) * per, unroll=2)
        def _(h):
            c, s = cols(h + heads), cols(h)
            keys = jnp.concatenate([kv_in[0, :, s], k[0, lower, c]], axis=0)
            values = jnp.concatenate([kv_in[1, :, s], v[0, lower, c]], axis=0)
            dq, dk, dv = attend_back(q[0, lower, c], keys, values, g[0, lower, c], half)
            gq[0, lower, c] = dq.astype(BF16)
            gk[0, lower, c] = dk[half:].astype(BF16)
            gv[0, lower, c] = dv[half:].astype(BF16)
            ret_out[0, :, s] = dk[:half].astype(BF16)
            ret_out[1, :, s] = dv[:half].astype(BF16)

        span = pl.ds(chunk * per * HEAD_FEATURES, per * HEAD_FEATURES)
        for i in range(2):
            at = chunk * 2 + i
            copy = remote(
                ret_out.at[i, :, span], ret_in.at[i, :, span], ret_send.at[at], ret_recv.at[at],
                {"seq": left, "dp": dp},
            )
            copy.start()
            ret_copies.append(copy)

    down_all = jnp.concatenate([down_w[p].astype(F32) for p in range(3)], axis=0).astype(BF16)
    projected = dot(down_all, tok[0], ((1,), (1,)))
    ranks = down_w.shape[1]
    returned, ups = [], []
    for p, ref in enumerate((gq, gk, gv)):
        if p == 1:
            for copy in ret_copies:
                copy.wait_recv()
            gk[0, upper, shifted] = (part[0] + ret_in[0].astype(F32)).astype(BF16)
            gv[0, upper, shifted] = (part[1] + ret_in[1].astype(F32)).astype(BF16)
        grad = ref[0]
        returned.append(dot(up_w[p], grad, ((1,), (1,))))
        ups.append(dot(projected[p * ranks:(p + 1) * ranks].astype(BF16), grad, ((1,), (0,))))
    downs = dot(jnp.concatenate(returned, axis=0).astype(BF16), tok[0], ((1,), (0,)))
    ups = jnp.concatenate(ups, axis=0)

    wd, wu = model_width // n_plane, width // n_plane
    wide = (wd + wu) // 2
    for c in range(n_plane):
        rs_out[c] = jnp.concatenate(
            [
                downs[:, c * wd:c * wd + wide],
                jnp.concatenate(
                    [downs[:, c * wd + wide:(c + 1) * wd], ups[:, c * wu:(c + 1) * wu]], axis=1
                ),
            ],
            axis=0,
        ).astype(BF16)
    copies = []
    for j in range(1, n_plane):
        c, target = plane_id(j)
        copy = remote(rs_out.at[c], rs_in.at[mine], rs_send.at[j], rs_recv.at[j], target)
        copy.start()
        copies.append(copy)
    total = rs_out[mine].astype(F32)
    for j in range(1, n_plane):
        c = lax.rem(mine + n_plane - j, n_plane)
        remote(rs_out.at[c], rs_in.at[c], rs_send.at[j], rs_recv.at[j], plane_id(j)[1]).wait_recv()
        total = total + rs_in[c].astype(F32)
    zbuf[zone] = total.astype(BF16)
    for j in range(1, n_z):
        _, target = zone_id(j)
        copy = remote(zbuf.at[zone], zbuf.at[zone], z_send.at[j], z_recv.at[j], target)
        copy.start()
        copies.append(copy)
    for j in range(1, n_z):
        z = lax.rem(zone + n_z - j, n_z)
        remote(zbuf.at[z], zbuf.at[z], z_send.at[j], z_recv.at[j], zone_id(j)[1]).wait_recv()
    total = zbuf[0].astype(F32)
    for z in range(1, n_z):
        total = total + zbuf[z].astype(F32)
    factor = ADAPTER_SCALE / math.sqrt(rows * n_seq * n_dp)
    gbuf[mine] = (total * factor).astype(BF16)
    for j in range(1, n_plane):
        _, target = plane_id(j)
        copy = remote(gbuf.at[mine], gbuf.at[mine], ag_send.at[j], ag_recv.at[j], target)
        copy.start()
        copies.append(copy)
    for j in range(1, n_plane):
        c = lax.rem(mine + n_plane - j, n_plane)
        remote(gbuf.at[c], gbuf.at[c], ag_send.at[j], ag_recv.at[j], plane_id(j)[1]).wait_recv()
    gbuf_out[...] = gbuf[...]
    for copy in kv_copies + ret_copies + copies:
        copy.wait_send()


def finish(n_plane, gq_in, gk_in, gv_in, sums, gq, gk, gv, gd, gu, down, up, sems):
    copies = [
        pltpu.make_async_copy(src, dst, sems.at[i])
        for i, (src, dst) in enumerate(((gq_in, gq), (gk_in, gk), (gv_in, gv)))
    ]
    for copy in copies:
        copy.start()
    projections, ranks, model_width = down.shape
    wd, wu = model_width // n_plane, up.shape[2] // n_plane
    wide = (wd + wu) // 2
    n = projections * ranks
    for c in range(n_plane):
        both = sums[c].astype(F32)
        for p in range(projections):
            at = p * ranks
            down[p, :, c * wd:c * wd + wide] = both[at:at + ranks]
            down[p, :, c * wd + wide:(c + 1) * wd] = both[n + at:n + at + ranks, :wd - wide]
            up[p, :, c * wu:(c + 1) * wu] = both[n + at:n + at + ranks, wd - wide:]
    last = [
        pltpu.make_async_copy(down, gd, sems.at[3]), pltpu.make_async_copy(up, gu, sems.at[4])
    ]
    for copy in last:
        copy.start()
    for copy in copies + last:
        copy.wait()


def shards(n_seq, n_dp, tokens, query, key, value, gradient, down_w, up_w):
    _, rows, width = query.shape
    half, half_width = rows // 2, width // 2
    projections, ranks, model_width = down_w.shape
    n_plane, n_z = n_dp * PLANE_SEQ, n_seq // PLANE_SEQ
    piece = (2 * projections * ranks, (model_width + width) // n_plane // 2)
    dma = pltpu.SemaphoreType.DMA
    vmem = pl.BlockSpec(memory_space=pltpu.VMEM)
    *grads, sums = pl.pallas_call(
        functools.partial(kernel, n_seq, n_dp),
        out_shape=[jax.ShapeDtypeStruct(query.shape, BF16)] * 3
        + [jax.ShapeDtypeStruct((n_plane,) + piece, BF16)],
        in_specs=[vmem] * 7,
        out_specs=[vmem] * 4,
        scratch_shapes=[
            pltpu.VMEM((2, half, half_width), BF16),
            pltpu.VMEM((2, half, half_width), BF16),
            pltpu.VMEM((2, half, half_width), BF16),
            pltpu.VMEM((2, half, half_width), F32),
            pltpu.VMEM((n_plane,) + piece, BF16),
            pltpu.VMEM((n_plane,) + piece, BF16),
            pltpu.VMEM((n_z,) + piece, BF16),
            pltpu.VMEM((n_plane,) + piece, BF16),
            dma((2,)), dma((2,)), dma((4,)), dma((4,)),
            dma((n_plane,)), dma((n_plane,)), dma((n_z,)), dma((n_z,)),
            dma((n_plane,)), dma((n_plane,)),
        ],
        compiler_params=pltpu.CompilerParams(
            collective_id=0, has_side_effects=True, vmem_limit_bytes=36 * 1024 * 1024
        ),
    )(tokens, query, key, value, gradient, down_w, up_w)
    anywhere = pl.BlockSpec(memory_space=pl.ANY)
    return pl.pallas_call(
        functools.partial(finish, n_plane),
        out_shape=[jax.ShapeDtypeStruct(query.shape, BF16)] * 3
        + [jax.ShapeDtypeStruct(down_w.shape, F32), jax.ShapeDtypeStruct(up_w.shape, F32)],
        in_specs=[anywhere] * 3 + [vmem],
        out_specs=[anywhere] * 5,
        scratch_shapes=[
            pltpu.VMEM(down_w.shape, F32), pltpu.VMEM(up_w.shape, F32), dma((5,)),
        ],
        compiler_params=pltpu.CompilerParams(vmem_limit_bytes=8 * 1024 * 1024),
    )(*grads, sums)


def solution(mesh):
    split = P("dp", "seq", None)
    return jax.shard_map(
        functools.partial(shards, mesh.shape["seq"], mesh.shape["dp"]),
        mesh=mesh,
        in_specs=(split,) * 5 + (P(), P()),
        out_specs=(split,) * 3 + (P(), P()),
        check_vma=False,
    )
```

```python
import functools
import math

import jax
import jax.numpy as jnp
from jax import lax
from jax.experimental import pallas as pl
from jax.experimental.pallas import tpu as pltpu
from jax.sharding import PartitionSpec as P

HEAD_FEATURES = 128
ADAPTER_SCALE = 2.0
PLANE_SEQ = 4
F32 = jnp.float32
BF16 = jnp.bfloat16
MESH = pl.DeviceIdType.MESH


def dot(a, b, dims):
    return lax.dot_general(a, b, (dims, ((), ())), preferred_element_type=F32)


def attend_back(query, key, value, gradient, offset):
    scale = 1.0 / math.sqrt(HEAD_FEATURES)
    scores = dot(key, query, ((1,), (1,)))
    shape = scores.shape
    keep = lax.broadcasted_iota(jnp.int32, shape, 0) <= (
        lax.broadcasted_iota(jnp.int32, shape, 1) + offset
    )
    scores = jnp.where(keep, scores, -jnp.inf)
    highest = jnp.max(scores, axis=0, keepdims=True)
    raised = jnp.exp2((scores - highest) * (scale * math.log2(math.e)))
    weights = raised * (1.0 / jnp.sum(raised, axis=0, keepdims=True))
    weights_low = weights.astype(BF16)
    grad_weights = dot(value, gradient, ((1,), (1,)))
    row_dots = jnp.sum(weights_low.astype(F32) * grad_weights, axis=0, keepdims=True)
    grad_scores = (weights * (grad_weights - row_dots)).astype(BF16)
    grad_value = dot(weights_low, gradient, ((1,), (0,)))
    grad_key = dot(grad_scores, query, ((1,), (0,))) * scale
    grad_query = dot(grad_scores, key, ((0,), (0,))) * scale
    return grad_query, grad_key, grad_value


def kernel(
    n_seq, n_dp, tok_hbm, q_hbm, k_hbm, v_hbm, g_hbm, down_hbm, up_hbm, gq_hbm, gk_hbm, gv_hbm, first_out, last_out,
    gq, gk, gv, tok, q, k, v, g, down_w, up_w, kv_in, ret_out, ret_in, part,
    rs_out0, rs_in0, zbuf0, gbuf0, rs_out1, rs_in1, zbuf1, gbuf1,
    load_sem, store_sem, kv_send, kv_recv, ret_send, ret_recv,
    rs_send, rs_recv, z_send, z_recv, ag_send, ag_recv,
):
    rows, width = q.shape[1:]
    model_width = tok.shape[2]
    half, half_width = rows // 2, width // 2
    heads = half_width // HEAD_FEATURES
    seq, dp = lax.axis_index("seq"), lax.axis_index("dp")
    right, left = lax.rem(seq + 1, n_seq), lax.rem(seq + n_seq - 1, n_seq)
    n_plane, n_z = n_dp * PLANE_SEQ, n_seq // PLANE_SEQ
    mine, zone = dp * PLANE_SEQ + lax.rem(seq, PLANE_SEQ), seq // PLANE_SEQ

    def plane_id(j):
        c = lax.rem(mine + j, n_plane)
        return c, {"seq": zone * PLANE_SEQ + lax.rem(c, PLANE_SEQ), "dp": c // PLANE_SEQ}

    def zone_id(j):
        z = lax.rem(zone + j, n_z)
        return z, {"seq": z * PLANE_SEQ + lax.rem(seq, PLANE_SEQ), "dp": dp}

    def remote(src, dst, send, recv, target):
        return pltpu.make_async_remote_copy(
            src_ref=src, dst_ref=dst, send_sem=send, recv_sem=recv,
            device_id=target, device_id_type=MESH,
        )

    loads = [
        pltpu.make_async_copy(src, dst, load_sem.at[i])
        for i, (src, dst) in enumerate(
            ((q_hbm, q), (k_hbm, k), (v_hbm, v), (g_hbm, g),
             (down_hbm, down_w), (up_hbm, up_w), (tok_hbm, tok))
        )
    ]
    for copy in loads:
        copy.start()
    barrier = pltpu.get_barrier_semaphore()
    targets = [{"seq": left, "dp": dp}, {"seq": right, "dp": dp}]
    targets += [plane_id(j)[1] for j in range(1, n_plane)]
    targets += [zone_id(j)[1] for j in range(1, n_z)]
    for target in targets:
        pl.semaphore_signal(barrier, inc=1, device_id=target, device_id_type=MESH)
    pl.semaphore_wait(barrier, len(targets))

    upper, lower = pl.ds(half, half), pl.ds(0, half)
    shifted = pl.ds(half_width, half_width)
    kv_copies = [
        remote(
            ref.at[0, upper, shifted], kv_in.at[i], kv_send.at[i], kv_recv.at[i],
            {"seq": right, "dp": dp},
        )
        for i, ref in enumerate((k_hbm, v_hbm))
    ]
    for copy in kv_copies:
        copy.start()
    for copy in loads[:4]:
        copy.wait()

    def cols(h):
        return pl.ds(pl.multiple_of(h * HEAD_FEATURES, HEAD_FEATURES), HEAD_FEATURES)

    @pl.loop(0, heads, unroll=2)
    def _(h):
        c = cols(h)
        dq, dk, dv = attend_back(q[0, :, c], k[0, :, c], v[0, :, c], g[0, :, c], 0)
        gq[0, :, c] = dq.astype(BF16)
        gk[0, :, c] = dk.astype(BF16)
        gv[0, :, c] = dv.astype(BF16)

    @pl.loop(0, heads, unroll=4)
    def _(h):
        c, s = cols(h + heads), cols(h)
        dq, dk, dv = attend_back(
            q[0, upper, c], k[0, upper, c], v[0, upper, c], g[0, upper, c], 0
        )
        gq[0, upper, c] = dq.astype(BF16)
        part[0, :, s] = dk
        part[1, :, s] = dv

    for copy in kv_copies:
        copy.wait_recv()
    ret_copies = []
    chunks = ret_send.shape[0] // 2
    per = heads // chunks
    for chunk in range(chunks):
        @pl.loop(chunk * per, (chunk + 1) * per, unroll=2)
        def _(h):
            c, s = cols(h + heads), cols(h)
            keys = jnp.concatenate([kv_in[0, :, s], k[0, lower, c]], axis=0)
            values = jnp.concatenate([kv_in[1, :, s], v[0, lower, c]], axis=0)
            dq, dk, dv = attend_back(q[0, lower, c], keys, values, g[0, lower, c], half)
            gq[0, lower, c] = dq.astype(BF16)
            gk[0, lower, c] = dk[half:].astype(BF16)
            gv[0, lower, c] = dv[half:].astype(BF16)
            ret_out[0, :, s] = dk[:half].astype(BF16)
            ret_out[1, :, s] = dv[:half].astype(BF16)

        span = pl.ds(chunk * per * HEAD_FEATURES, per * HEAD_FEATURES)
        for i in range(2):
            at = chunk * 2 + i
            copy = remote(
                ret_out.at[i, :, span], ret_in.at[i, :, span], ret_send.at[at], ret_recv.at[at],
                {"seq": left, "dp": dp},
            )
            copy.start()
            ret_copies.append(copy)

    for copy in loads[4:]:
        copy.wait()
    ranks = down_w.shape[1]
    wd, wu = model_width // n_plane, width // n_plane
    wide = (wd + wu) // 2
    factor = ADAPTER_SCALE / math.sqrt(rows * n_seq * n_dp)
    buffers = ((rs_out0, rs_in0, zbuf0, gbuf0), (rs_out1, rs_in1, zbuf1, gbuf1))
    copies = []
    stores = [
        pltpu.make_async_copy(src, dst, store_sem.at[i])
        for i, (src, dst) in enumerate(((gq, gq_hbm), (gk, gk_hbm), (gv, gv_hbm)))
    ]
    stores[0].start()

    def scatter(group, downs, ups):
        rs_out, rs_in, _, _ = buffers[group]
        for c in range(n_plane):
            tail = [downs[:, c * wd + wide:(c + 1) * wd], ups[:, c * wu:(c + 1) * wu]]
            rs_out[c] = jnp.concatenate(
                [downs[:, c * wd:c * wd + wide], jnp.concatenate(tail, axis=1)], axis=0
            ).astype(BF16)
        for j in range(1, n_plane):
            c, target = plane_id(j)
            copy = remote(
                rs_out.at[c], rs_in.at[mine], rs_send.at[group, j], rs_recv.at[group, j], target
            )
            copy.start()
            copies.append(copy)

    def exchange(group):
        rs_out, rs_in, zbuf, _ = buffers[group]
        total = rs_out[mine].astype(F32)
        for j in range(1, n_plane):
            c = lax.rem(mine + n_plane - j, n_plane)
            remote(
                rs_out.at[c], rs_in.at[c], rs_send.at[group, j], rs_recv.at[group, j],
                plane_id(j)[1],
            ).wait_recv()
            total = total + rs_in[c].astype(F32)
        zbuf[zone] = total.astype(BF16)
        for j in range(1, n_z):
            copy = remote(
                zbuf.at[zone], zbuf.at[zone], z_send.at[group, j], z_recv.at[group, j],
                zone_id(j)[1],
            )
            copy.start()
            copies.append(copy)

    def gather(group):
        _, _, zbuf, gbuf = buffers[group]
        for j in range(1, n_z):
            z = lax.rem(zone + n_z - j, n_z)
            remote(
                zbuf.at[z], zbuf.at[z], z_send.at[group, j], z_recv.at[group, j], zone_id(j)[1]
            ).wait_recv()
        total = zbuf[0].astype(F32)
        for z in range(1, n_z):
            total = total + zbuf[z].astype(F32)
        gbuf[mine] = (total * factor).astype(BF16)
        for j in range(1, n_plane):
            copy = remote(
                gbuf.at[mine], gbuf.at[mine], ag_send.at[group, j], ag_recv.at[group, j],
                plane_id(j)[1],
            )
            copy.start()
            copies.append(copy)

    def collect(group, out):
        gbuf = buffers[group][3]
        for j in range(1, n_plane):
            c = lax.rem(mine + n_plane - j, n_plane)
            remote(
                gbuf.at[c], gbuf.at[c], ag_send.at[group, j], ag_recv.at[group, j], plane_id(j)[1]
            ).wait_recv()
        out[...] = gbuf[...]

    down_all = jnp.concatenate([down_w[p].astype(F32) for p in range(3)], axis=0).astype(BF16)
    projected = dot(down_all, tok[0], ((1,), (1,)))

    def adapters(parts):
        returned, ups = [], []
        for p, ref in parts:
            grad = ref[0]
            returned.append(dot(up_w[p], grad, ((1,), (1,))))
            mid = projected[p * ranks:(p + 1) * ranks].astype(BF16)
            ups.append(dot(mid, grad, ((1,), (0,))))
        downs = dot(jnp.concatenate(returned, axis=0).astype(BF16), tok[0], ((1,), (0,)))
        return downs, jnp.concatenate(ups, axis=0)

    scatter(0, *adapters(((0, gq),)))
    exchange(0)
    for copy in ret_copies:
        copy.wait_recv()
    gk[0, upper, shifted] = (part[0] + ret_in[0].astype(F32)).astype(BF16)
    gv[0, upper, shifted] = (part[1] + ret_in[1].astype(F32)).astype(BF16)
    for copy in stores[1:]:
        copy.start()
    scatter(1, *adapters(((1, gk), (2, gv))))
    gather(0)
    exchange(1)
    collect(0, first_out)
    gather(1)
    collect(1, last_out)
    for copy in stores:
        copy.wait()
    for copy in kv_copies + ret_copies + copies:
        copy.wait_send()


def finish(n_plane, gq_in, gk_in, gv_in, first, last_two, gq, gk, gv, gd, gu, down, up, sems):
    copies = [
        pltpu.make_async_copy(src, dst, sems.at[i])
        for i, (src, dst) in enumerate(((gq_in, gq), (gk_in, gk), (gv_in, gv)))
    ]
    for copy in copies:
        copy.start()
    projections, ranks, model_width = down.shape
    wd, wu = model_width // n_plane, up.shape[2] // n_plane
    wide = (wd + wu) // 2
    for sums, start, count in ((first, 0, 1), (last_two, 1, projections - 1)):
        n = count * ranks
        for c in range(n_plane):
            both = sums[c].astype(F32)
            for p in range(count):
                top = both[p * ranks:(p + 1) * ranks]
                low = both[n + p * ranks:n + (p + 1) * ranks]
                down[start + p, :, c * wd:c * wd + wide] = top
                down[start + p, :, c * wd + wide:(c + 1) * wd] = low[:, :wd - wide]
                up[start + p, :, c * wu:(c + 1) * wu] = low[:, wd - wide:]
    last = [
        pltpu.make_async_copy(down, gd, sems.at[3]), pltpu.make_async_copy(up, gu, sems.at[4])
    ]
    for copy in last:
        copy.start()
    for copy in copies + last:
        copy.wait()


def shards(n_seq, n_dp, tokens, query, key, value, gradient, down_w, up_w):
    _, rows, width = query.shape
    half, half_width = rows // 2, width // 2
    projections, ranks, model_width = down_w.shape
    n_plane, n_z = n_dp * PLANE_SEQ, n_seq // PLANE_SEQ
    across = (model_width + width) // n_plane // 2
    first, last_two = (2 * ranks, across), (2 * (projections - 1) * ranks, across)
    dma = pltpu.SemaphoreType.DMA
    anywhere = pl.BlockSpec(memory_space=pl.ANY)
    vmem = pl.BlockSpec(memory_space=pltpu.VMEM)
    *grads, first_sums, last_sums = pl.pallas_call(
        functools.partial(kernel, n_seq, n_dp),
        out_shape=[jax.ShapeDtypeStruct(query.shape, BF16)] * 3
        + [jax.ShapeDtypeStruct((n_plane,) + piece, BF16) for piece in (first, last_two)],
        in_specs=[anywhere] * 7,
        out_specs=[anywhere] * 3 + [vmem] * 2,
        scratch_shapes=[
            pltpu.VMEM(ref.shape, BF16)
            for ref in (query, query, query, tokens, query, key, value, gradient, down_w, up_w)
        ]
        + [pltpu.VMEM((2, half, half_width), BF16)] * 3
        + [pltpu.VMEM((2, half, half_width), F32)]
        + [
            pltpu.VMEM((n,) + piece, BF16)
            for piece in (first, last_two)
            for n in (n_plane, n_plane, n_z, n_plane)
        ]
        + [dma((7,)), dma((3,)), dma((2,)), dma((2,)), dma((4,)), dma((4,))]
        + [dma((2, n)) for n in (n_plane, n_plane, n_z, n_z, n_plane, n_plane)],
        compiler_params=pltpu.CompilerParams(
            collective_id=0, has_side_effects=True, vmem_limit_bytes=58 * 1024 * 1024
        ),
    )(tokens, query, key, value, gradient, down_w, up_w)
    return pl.pallas_call(
        functools.partial(finish, n_plane),
        out_shape=[jax.ShapeDtypeStruct(query.shape, BF16)] * 3
        + [jax.ShapeDtypeStruct(down_w.shape, F32), jax.ShapeDtypeStruct(up_w.shape, F32)],
        in_specs=[anywhere] * 3 + [vmem] * 2,
        out_specs=[anywhere] * 5,
        scratch_shapes=[
            pltpu.VMEM(down_w.shape, F32), pltpu.VMEM(up_w.shape, F32), dma((5,)),
        ],
        compiler_params=pltpu.CompilerParams(vmem_limit_bytes=58 * 1024 * 1024),
    )(*grads, first_sums, last_sums)


def solution(mesh):
    split = P("dp", "seq", None)
    return jax.shard_map(
        functools.partial(shards, mesh.shape["seq"], mesh.shape["dp"]),
        mesh=mesh,
        in_specs=(split,) * 5 + (P(), P()),
        out_specs=(split,) * 3 + (P(), P()),
        check_vma=False,
    )
```

```python
import functools
import math

import jax
import jax.numpy as jnp
from jax import lax
from jax.experimental import pallas as pl
from jax.experimental.pallas import tpu as pltpu
from jax.sharding import PartitionSpec as P

HEAD_FEATURES = 128
ADAPTER_SCALE = 2.0
PLANE_SEQ = 4
F32 = jnp.float32
BF16 = jnp.bfloat16
MESH = pl.DeviceIdType.MESH


def dot(a, b, dims):
    return lax.dot_general(a, b, (dims, ((), ())), preferred_element_type=F32)


def attend_back(query, key, value, gradient, offset):
    scale = 1.0 / math.sqrt(HEAD_FEATURES)
    scores = dot(key, query, ((1,), (1,)))
    shape = scores.shape
    keep = lax.broadcasted_iota(jnp.int32, shape, 0) <= (
        lax.broadcasted_iota(jnp.int32, shape, 1) + offset
    )
    scores = jnp.where(keep, scores, -jnp.inf)
    highest = jnp.max(scores, axis=0, keepdims=True)
    raised = jnp.exp2((scores - highest) * (scale * math.log2(math.e)))
    weights = raised * (1.0 / jnp.sum(raised, axis=0, keepdims=True))
    weights_low = weights.astype(BF16)
    grad_weights = dot(value, gradient, ((1,), (1,)))
    row_dots = jnp.sum(weights_low.astype(F32) * grad_weights, axis=0, keepdims=True)
    grad_scores = (weights * (grad_weights - row_dots)).astype(BF16)
    grad_value = dot(weights_low, gradient, ((1,), (0,)))
    grad_key = dot(grad_scores, query, ((1,), (0,))) * scale
    grad_query = dot(grad_scores, key, ((0,), (0,))) * scale
    return grad_query, grad_key, grad_value


def kernel(
    n_seq, n_dp, tok_hbm, q_hbm, k_hbm, v_hbm, g_hbm, down_hbm, up_hbm, gq_hbm, gk_hbm, gv_hbm, first_out, last_out,
    gq, gk, gv, tok, q, k, v, g, down_w, up_w, kv_in, ret_out, ret_in, part,
    rs_out0, rs_in0, zbuf0, gbuf0, rs_out1, rs_in1, zbuf1, gbuf1,
    load_sem, store_sem, kv_send, kv_recv, ret_send, ret_recv,
    rs_send, rs_recv, z_send, z_recv, ag_send, ag_recv,
):
    rows, width = q.shape[1:]
    model_width = tok.shape[2]
    half, half_width = rows // 2, width // 2
    heads = half_width // HEAD_FEATURES
    seq, dp = lax.axis_index("seq"), lax.axis_index("dp")
    right, left = lax.rem(seq + 1, n_seq), lax.rem(seq + n_seq - 1, n_seq)
    n_plane, n_z = n_dp * PLANE_SEQ, n_seq // PLANE_SEQ
    mine, zone = dp * PLANE_SEQ + lax.rem(seq, PLANE_SEQ), seq // PLANE_SEQ

    def plane_id(j):
        c = lax.rem(mine + j, n_plane)
        return c, {"seq": zone * PLANE_SEQ + lax.rem(c, PLANE_SEQ), "dp": c // PLANE_SEQ}

    def zone_id(j):
        z = lax.rem(zone + j, n_z)
        return z, {"seq": z * PLANE_SEQ + lax.rem(seq, PLANE_SEQ), "dp": dp}

    def remote(src, dst, send, recv, target):
        return pltpu.make_async_remote_copy(
            src_ref=src, dst_ref=dst, send_sem=send, recv_sem=recv,
            device_id=target, device_id_type=MESH,
        )

    loads = [
        pltpu.make_async_copy(src, dst, load_sem.at[i])
        for i, (src, dst) in enumerate(
            ((q_hbm, q), (k_hbm, k), (v_hbm, v), (g_hbm, g),
             (down_hbm, down_w), (up_hbm, up_w), (tok_hbm, tok))
        )
    ]
    for copy in loads:
        copy.start()
    barrier = pltpu.get_barrier_semaphore()
    targets = [{"seq": left, "dp": dp}, {"seq": right, "dp": dp}]
    targets += [plane_id(j)[1] for j in range(1, n_plane)]
    targets += [zone_id(j)[1] for j in range(1, n_z)]
    for target in targets:
        pl.semaphore_signal(barrier, inc=1, device_id=target, device_id_type=MESH)
    pl.semaphore_wait(barrier, len(targets))

    upper, lower = pl.ds(half, half), pl.ds(0, half)
    shifted = pl.ds(half_width, half_width)
    chunks = kv_send.shape[0] // 2
    per = half_width // chunks
    kv_copies = [
        remote(
            ref.at[0, upper, pl.ds(half_width + chunk * per, per)],
            kv_in.at[i, :, pl.ds(chunk * per, per)],
            kv_send.at[chunk * 2 + i], kv_recv.at[chunk * 2 + i], {"seq": right, "dp": dp},
        )
        for chunk in range(chunks)
        for i, ref in enumerate((k_hbm, v_hbm))
    ]
    for copy in kv_copies:
        copy.start()
    for copy in loads[:4]:
        copy.wait()

    def cols(h):
        return pl.ds(pl.multiple_of(h * HEAD_FEATURES, HEAD_FEATURES), HEAD_FEATURES)

    @pl.loop(0, heads, unroll=2)
    def _(h):
        c = cols(h)
        dq, dk, dv = attend_back(q[0, :, c], k[0, :, c], v[0, :, c], g[0, :, c], 0)
        gq[0, :, c] = dq.astype(BF16)
        gk[0, :, c] = dk.astype(BF16)
        gv[0, :, c] = dv.astype(BF16)

    @pl.loop(0, heads, unroll=4)
    def _(h):
        c, s = cols(h + heads), cols(h)
        dq, dk, dv = attend_back(
            q[0, upper, c], k[0, upper, c], v[0, upper, c], g[0, upper, c], 0
        )
        gq[0, upper, c] = dq.astype(BF16)
        part[0, :, s] = dk
        part[1, :, s] = dv

    ret_copies = []
    some = heads // chunks
    for chunk in range(chunks):
        for i in range(2):
            kv_copies[chunk * 2 + i].wait_recv()

        @pl.loop(chunk * some, (chunk + 1) * some, unroll=2)
        def _(h):
            c, s = cols(h + heads), cols(h)
            keys = jnp.concatenate([kv_in[0, :, s], k[0, lower, c]], axis=0)
            values = jnp.concatenate([kv_in[1, :, s], v[0, lower, c]], axis=0)
            dq, dk, dv = attend_back(q[0, lower, c], keys, values, g[0, lower, c], half)
            gq[0, lower, c] = dq.astype(BF16)
            gk[0, lower, c] = dk[half:].astype(BF16)
            gv[0, lower, c] = dv[half:].astype(BF16)
            ret_out[0, :, s] = dk[:half].astype(BF16)
            ret_out[1, :, s] = dv[:half].astype(BF16)

        span = pl.ds(chunk * per, per)
        for i in range(2):
            at = chunk * 2 + i
            copy = remote(
                ret_out.at[i, :, span], ret_in.at[i, :, span], ret_send.at[at], ret_recv.at[at],
                {"seq": left, "dp": dp},
            )
            copy.start()
            ret_copies.append(copy)

    for copy in loads[4:]:
        copy.wait()
    ranks = down_w.shape[1]
    wd, wu = model_width // n_plane, width // n_plane
    wide = (wd + wu) // 2
    factor = ADAPTER_SCALE / math.sqrt(rows * n_seq * n_dp)
    buffers = ((rs_out0, rs_in0, zbuf0, gbuf0), (rs_out1, rs_in1, zbuf1, gbuf1))
    copies = []
    stores = [
        pltpu.make_async_copy(src, dst, store_sem.at[i])
        for i, (src, dst) in enumerate(((gq, gq_hbm), (gk, gk_hbm), (gv, gv_hbm)))
    ]
    stores[0].start()

    def scatter(group, downs, ups):
        rs_out, rs_in, _, _ = buffers[group]
        for c in range(n_plane):
            tail = [downs[:, c * wd + wide:(c + 1) * wd], ups[:, c * wu:(c + 1) * wu]]
            rs_out[c] = jnp.concatenate(
                [downs[:, c * wd:c * wd + wide], jnp.concatenate(tail, axis=1)], axis=0
            ).astype(BF16)
        for j in range(1, n_plane):
            c, target = plane_id(j)
            copy = remote(
                rs_out.at[c], rs_in.at[mine], rs_send.at[group, j], rs_recv.at[group, j], target
            )
            copy.start()
            copies.append(copy)

    def exchange(group):
        rs_out, rs_in, zbuf, _ = buffers[group]
        total = rs_out[mine].astype(F32)
        for j in range(1, n_plane):
            c = lax.rem(mine + n_plane - j, n_plane)
            remote(
                rs_out.at[c], rs_in.at[c], rs_send.at[group, j], rs_recv.at[group, j],
                plane_id(j)[1],
            ).wait_recv()
            total = total + rs_in[c].astype(F32)
        zbuf[zone] = total.astype(BF16)
        for j in range(1, n_z):
            copy = remote(
                zbuf.at[zone], zbuf.at[zone], z_send.at[group, j], z_recv.at[group, j],
                zone_id(j)[1],
            )
            copy.start()
            copies.append(copy)

    def gather(group):
        _, _, zbuf, gbuf = buffers[group]
        for j in range(1, n_z):
            z = lax.rem(zone + n_z - j, n_z)
            remote(
                zbuf.at[z], zbuf.at[z], z_send.at[group, j], z_recv.at[group, j], zone_id(j)[1]
            ).wait_recv()
        total = zbuf[0].astype(F32)
        for z in range(1, n_z):
            total = total + zbuf[z].astype(F32)
        gbuf[mine] = (total * factor).astype(BF16)
        for j in range(1, n_plane):
            copy = remote(
                gbuf.at[mine], gbuf.at[mine], ag_send.at[group, j], ag_recv.at[group, j],
                plane_id(j)[1],
            )
            copy.start()
            copies.append(copy)

    def collect(group, out):
        gbuf = buffers[group][3]
        for j in range(1, n_plane):
            c = lax.rem(mine + n_plane - j, n_plane)
            remote(
                gbuf.at[c], gbuf.at[c], ag_send.at[group, j], ag_recv.at[group, j], plane_id(j)[1]
            ).wait_recv()
        out[...] = gbuf[...]

    down_all = jnp.concatenate([down_w[p].astype(F32) for p in range(3)], axis=0).astype(BF16)
    projected = dot(down_all, tok[0], ((1,), (1,)))

    def adapters(parts):
        returned, ups = [], []
        for p, ref in parts:
            grad = ref[0]
            returned.append(dot(up_w[p], grad, ((1,), (1,))))
            mid = projected[p * ranks:(p + 1) * ranks].astype(BF16)
            ups.append(dot(mid, grad, ((1,), (0,))))
        downs = dot(jnp.concatenate(returned, axis=0).astype(BF16), tok[0], ((1,), (0,)))
        return downs, jnp.concatenate(ups, axis=0)

    scatter(0, *adapters(((0, gq),)))
    exchange(0)
    for copy in ret_copies:
        copy.wait_recv()
    gk[0, upper, shifted] = (part[0] + ret_in[0].astype(F32)).astype(BF16)
    gv[0, upper, shifted] = (part[1] + ret_in[1].astype(F32)).astype(BF16)
    for copy in stores[1:]:
        copy.start()
    scatter(1, *adapters(((1, gk), (2, gv))))
    gather(0)
    exchange(1)
    collect(0, first_out)
    gather(1)
    collect(1, last_out)
    for copy in stores:
        copy.wait()
    for copy in kv_copies + ret_copies + copies:
        copy.wait_send()


def finish(
    n_plane, gq_in, gk_in, gv_in, first, last_two, gq, gk, gv, gd, gu, down, up, held, load_sem, sems
):
    loads = [
        pltpu.make_async_copy(src, held.at[i], load_sem.at[i])
        for i, src in enumerate((gq_in, gk_in, gv_in))
    ]
    copies = [
        pltpu.make_async_copy(held.at[i], dst, sems.at[i]) for i, dst in enumerate((gq, gk, gv))
    ]
    for copy in loads:
        copy.start()
    for load, copy in zip(loads, copies):
        load.wait()
        copy.start()
    projections, ranks, model_width = down.shape
    wd, wu = model_width // n_plane, up.shape[2] // n_plane
    wide = (wd + wu) // 2
    for sums, start, count in ((first, 0, 1), (last_two, 1, projections - 1)):
        n = count * ranks
        for c in range(n_plane):
            both = sums[c].astype(F32)
            for p in range(count):
                top = both[p * ranks:(p + 1) * ranks]
                low = both[n + p * ranks:n + (p + 1) * ranks]
                down[start + p, :, c * wd:c * wd + wide] = top
                down[start + p, :, c * wd + wide:(c + 1) * wd] = low[:, :wd - wide]
                up[start + p, :, c * wu:(c + 1) * wu] = low[:, wd - wide:]
    last = [
        pltpu.make_async_copy(down, gd, sems.at[3]), pltpu.make_async_copy(up, gu, sems.at[4])
    ]
    for copy in last:
        copy.start()
    for copy in copies + last:
        copy.wait()


def shards(n_seq, n_dp, tokens, query, key, value, gradient, down_w, up_w):
    _, rows, width = query.shape
    half, half_width = rows // 2, width // 2
    projections, ranks, model_width = down_w.shape
    n_plane, n_z = n_dp * PLANE_SEQ, n_seq // PLANE_SEQ
    across = (model_width + width) // n_plane // 2
    first, last_two = (2 * ranks, across), (2 * (projections - 1) * ranks, across)
    dma = pltpu.SemaphoreType.DMA
    anywhere = pl.BlockSpec(memory_space=pl.ANY)
    vmem = pl.BlockSpec(memory_space=pltpu.VMEM)
    *grads, first_sums, last_sums = pl.pallas_call(
        functools.partial(kernel, n_seq, n_dp),
        out_shape=[jax.ShapeDtypeStruct(query.shape, BF16)] * 3
        + [jax.ShapeDtypeStruct((n_plane,) + piece, BF16) for piece in (first, last_two)],
        in_specs=[anywhere] * 7,
        out_specs=[anywhere] * 3 + [vmem] * 2,
        scratch_shapes=[
            pltpu.VMEM(ref.shape, BF16)
            for ref in (query, query, query, tokens, query, key, value, gradient, down_w, up_w)
        ]
        + [pltpu.VMEM((2, half, half_width), BF16)] * 3
        + [pltpu.VMEM((2, half, half_width), F32)]
        + [
            pltpu.VMEM((n,) + piece, BF16)
            for piece in (first, last_two)
            for n in (n_plane, n_plane, n_z, n_plane)
        ]
        + [dma((7,)), dma((3,))]
        + [dma((8,))] * 4
        + [dma((2, n)) for n in (n_plane, n_plane, n_z, n_z, n_plane, n_plane)],
        compiler_params=pltpu.CompilerParams(
            collective_id=0, has_side_effects=True, vmem_limit_bytes=58 * 1024 * 1024
        ),
    )(tokens, query, key, value, gradient, down_w, up_w)
    return pl.pallas_call(
        functools.partial(finish, n_plane),
        out_shape=[jax.ShapeDtypeStruct(query.shape, BF16)] * 3
        + [jax.ShapeDtypeStruct(down_w.shape, F32), jax.ShapeDtypeStruct(up_w.shape, F32)],
        in_specs=[anywhere] * 3 + [vmem] * 2,
        out_specs=[anywhere] * 5,
        scratch_shapes=[
            pltpu.VMEM(down_w.shape, F32), pltpu.VMEM(up_w.shape, F32),
            pltpu.VMEM((3,) + query.shape, BF16), dma((3,)), dma((5,)),
        ],
        compiler_params=pltpu.CompilerParams(vmem_limit_bytes=58 * 1024 * 1024),
    )(*grads, first_sums, last_sums)


def solution(mesh):
    split = P("dp", "seq", None)
    return jax.shard_map(
        functools.partial(shards, mesh.shape["seq"], mesh.shape["dp"]),
        mesh=mesh,
        in_specs=(split,) * 5 + (P(), P()),
        out_specs=(split,) * 3 + (P(), P()),
        check_vma=False,
    )
```

```python
import functools
import math

import jax
import jax.numpy as jnp
from jax import lax
from jax.experimental import pallas as pl
from jax.experimental.pallas import tpu as pltpu
from jax.sharding import PartitionSpec as P

HEAD_FEATURES = 128
ADAPTER_SCALE = 2.0
PLANE_SEQ = 4
F32 = jnp.float32
BF16 = jnp.bfloat16
MESH = pl.DeviceIdType.MESH


def dot(a, b, dims):
    return lax.dot_general(a, b, (dims, ((), ())), preferred_element_type=F32)


def attend_back(query, key, value, gradient, offset):
    scale = 1.0 / math.sqrt(HEAD_FEATURES)
    scores = dot(key, query, ((1,), (1,)))
    shape = scores.shape
    keep = lax.broadcasted_iota(jnp.int32, shape, 0) <= (
        lax.broadcasted_iota(jnp.int32, shape, 1) + offset
    )
    scores = jnp.where(keep, scores, -jnp.inf)
    highest = jnp.max(scores, axis=0, keepdims=True)
    raised = jnp.exp2((scores - highest) * (scale * math.log2(math.e)))
    weights = raised * (1.0 / jnp.sum(raised, axis=0, keepdims=True))
    weights_low = weights.astype(BF16)
    grad_weights = dot(value, gradient, ((1,), (1,)))
    row_dots = jnp.sum(weights_low.astype(F32) * grad_weights, axis=0, keepdims=True)
    grad_scores = (weights * (grad_weights - row_dots)).astype(BF16)
    grad_value = dot(weights_low, gradient, ((1,), (0,)))
    grad_key = dot(grad_scores, query, ((1,), (0,))) * scale
    grad_query = dot(grad_scores, key, ((0,), (0,))) * scale
    return grad_query, grad_key, grad_value


def kernel(
    n_seq, n_dp, tok_hbm, q_hbm, k_hbm, v_hbm, g_hbm, down_hbm, up_hbm, gq_hbm, gk_hbm, gv_hbm, first_out, last_out,
    gq, gk, gv, tok, q, k, v, g, down_w, up_w, kv_in, ret_out, ret_in, part,
    rs_out0, rs_in0, zbuf0, gbuf0, rs_out1, rs_in1, zbuf1, gbuf1,
    load_sem, store_sem, kv_send, kv_recv, ret_send, ret_recv,
    rs_send, rs_recv, z_send, z_recv, ag_send, ag_recv,
):
    rows, width = q.shape[1:]
    model_width = tok.shape[2]
    half, half_width = rows // 2, width // 2
    heads = half_width // HEAD_FEATURES
    seq, dp = lax.axis_index("seq"), lax.axis_index("dp")
    right, left = lax.rem(seq + 1, n_seq), lax.rem(seq + n_seq - 1, n_seq)
    n_plane, n_z = n_dp * PLANE_SEQ, n_seq // PLANE_SEQ
    mine, zone = dp * PLANE_SEQ + lax.rem(seq, PLANE_SEQ), seq // PLANE_SEQ

    def plane_id(j):
        c = lax.rem(mine + j, n_plane)
        return c, {"seq": zone * PLANE_SEQ + lax.rem(c, PLANE_SEQ), "dp": c // PLANE_SEQ}

    def zone_id(j):
        z = lax.rem(zone + j, n_z)
        return z, {"seq": z * PLANE_SEQ + lax.rem(seq, PLANE_SEQ), "dp": dp}

    def remote(src, dst, send, recv, target):
        return pltpu.make_async_remote_copy(
            src_ref=src, dst_ref=dst, send_sem=send, recv_sem=recv,
            device_id=target, device_id_type=MESH,
        )

    loads = [
        pltpu.make_async_copy(src, dst, load_sem.at[i])
        for i, (src, dst) in enumerate(
            ((q_hbm, q), (k_hbm, k), (v_hbm, v), (g_hbm, g),
             (down_hbm, down_w), (up_hbm, up_w), (tok_hbm, tok))
        )
    ]
    for copy in loads:
        copy.start()
    barrier = pltpu.get_barrier_semaphore()
    targets = [{"seq": left, "dp": dp}, {"seq": right, "dp": dp}]
    targets += [plane_id(j)[1] for j in range(1, n_plane)]
    targets += [zone_id(j)[1] for j in range(1, n_z)]
    for target in targets:
        pl.semaphore_signal(barrier, inc=1, device_id=target, device_id_type=MESH)
    pl.semaphore_wait(barrier, len(targets))

    upper, lower = pl.ds(half, half), pl.ds(0, half)
    shifted = pl.ds(half_width, half_width)
    chunks = kv_send.shape[0] // 2
    per = half_width // chunks
    kv_copies = [
        remote(
            ref.at[0, upper, pl.ds(half_width + chunk * per, per)],
            kv_in.at[i, :, pl.ds(chunk * per, per)],
            kv_send.at[chunk * 2 + i], kv_recv.at[chunk * 2 + i], {"seq": right, "dp": dp},
        )
        for chunk in range(chunks)
        for i, ref in enumerate((k_hbm, v_hbm))
    ]
    for copy in kv_copies:
        copy.start()
    for copy in loads[:4]:
        copy.wait()

    def cols(h):
        return pl.ds(pl.multiple_of(h * HEAD_FEATURES, HEAD_FEATURES), HEAD_FEATURES)

    @pl.loop(0, heads, unroll=2)
    def _(h):
        c = cols(h)
        dq, dk, dv = attend_back(q[0, :, c], k[0, :, c], v[0, :, c], g[0, :, c], 0)
        gq[0, :, c] = dq.astype(BF16)
        gk[0, :, c] = dk.astype(BF16)
        gv[0, :, c] = dv.astype(BF16)

    @pl.loop(0, heads, unroll=4)
    def _(h):
        c, s = cols(h + heads), cols(h)
        dq, dk, dv = attend_back(
            q[0, upper, c], k[0, upper, c], v[0, upper, c], g[0, upper, c], 0
        )
        gq[0, upper, c] = dq.astype(BF16)
        part[0, :, s] = dk
        part[1, :, s] = dv

    ret_copies = []
    some = heads // chunks
    for chunk in range(chunks):
        for i in range(2):
            kv_copies[chunk * 2 + i].wait_recv()

        @pl.loop(chunk * some, (chunk + 1) * some, unroll=2)
        def _(h):
            c, s = cols(h + heads), cols(h)
            keys = jnp.concatenate([kv_in[0, :, s], k[0, lower, c]], axis=0)
            values = jnp.concatenate([kv_in[1, :, s], v[0, lower, c]], axis=0)
            dq, dk, dv = attend_back(q[0, lower, c], keys, values, g[0, lower, c], half)
            gq[0, lower, c] = dq.astype(BF16)
            gk[0, lower, c] = dk[half:].astype(BF16)
            gv[0, lower, c] = dv[half:].astype(BF16)
            ret_out[0, :, s] = dk[:half].astype(BF16)
            ret_out[1, :, s] = dv[:half].astype(BF16)

        span = pl.ds(chunk * per, per)
        for i in range(2):
            at = chunk * 2 + i
            copy = remote(
                ret_out.at[i, :, span], ret_in.at[i, :, span], ret_send.at[at], ret_recv.at[at],
                {"seq": left, "dp": dp},
            )
            copy.start()
            ret_copies.append(copy)

    for copy in loads[4:]:
        copy.wait()
    ranks = down_w.shape[1]
    wd, wu = model_width // n_plane, width // n_plane
    wide = (wd + wu) // 2
    factor = ADAPTER_SCALE / math.sqrt(rows * n_seq * n_dp)
    buffers = ((rs_out0, rs_in0, zbuf0, gbuf0), (rs_out1, rs_in1, zbuf1, gbuf1))
    copies = []
    stores = [
        pltpu.make_async_copy(src, dst, store_sem.at[i])
        for i, (src, dst) in enumerate(((gq, gq_hbm), (gk, gk_hbm), (gv, gv_hbm)))
    ]
    stores[0].start()

    def scatter(group, downs, ups):
        rs_out, rs_in, _, _ = buffers[group]
        for c in range(n_plane):
            tail = [downs[:, c * wd + wide:(c + 1) * wd], ups[:, c * wu:(c + 1) * wu]]
            rs_out[c] = jnp.concatenate(
                [downs[:, c * wd:c * wd + wide], jnp.concatenate(tail, axis=1)], axis=0
            ).astype(BF16)
        for j in range(1, n_plane):
            c, target = plane_id(j)
            copy = remote(
                rs_out.at[c], rs_in.at[mine], rs_send.at[group, j], rs_recv.at[group, j], target
            )
            copy.start()
            copies.append(copy)

    def exchange(group):
        rs_out, rs_in, zbuf, _ = buffers[group]
        total = rs_out[mine].astype(F32)
        for j in range(1, n_plane):
            c = lax.rem(mine + n_plane - j, n_plane)
            remote(
                rs_out.at[c], rs_in.at[c], rs_send.at[group, j], rs_recv.at[group, j],
                plane_id(j)[1],
            ).wait_recv()
            total = total + rs_in[c].astype(F32)
        zbuf[zone] = total.astype(BF16)
        for j in range(1, n_z):
            copy = remote(
                zbuf.at[zone], zbuf.at[zone], z_send.at[group, j], z_recv.at[group, j],
                zone_id(j)[1],
            )
            copy.start()
            copies.append(copy)

    def gather(group):
        _, _, zbuf, gbuf = buffers[group]
        for j in range(1, n_z):
            z = lax.rem(zone + n_z - j, n_z)
            remote(
                zbuf.at[z], zbuf.at[z], z_send.at[group, j], z_recv.at[group, j], zone_id(j)[1]
            ).wait_recv()
        total = zbuf[0].astype(F32)
        for z in range(1, n_z):
            total = total + zbuf[z].astype(F32)
        gbuf[mine] = (total * factor).astype(BF16)
        for j in range(1, n_plane):
            copy = remote(
                gbuf.at[mine], gbuf.at[mine], ag_send.at[group, j], ag_recv.at[group, j],
                plane_id(j)[1],
            )
            copy.start()
            copies.append(copy)

    def collect(group, out):
        gbuf = buffers[group][3]
        for j in range(1, n_plane):
            c = lax.rem(mine + n_plane - j, n_plane)
            remote(
                gbuf.at[c], gbuf.at[c], ag_send.at[group, j], ag_recv.at[group, j], plane_id(j)[1]
            ).wait_recv()
        store = pltpu.make_async_copy(gbuf, out, store_sem.at[3 + group])
        store.start()
        stores.append(store)

    down_all = jnp.concatenate([down_w[p].astype(F32) for p in range(3)], axis=0).astype(BF16)
    projected = dot(down_all, tok[0], ((1,), (1,)))

    def adapters(parts):
        returned, ups = [], []
        for p, ref in parts:
            grad = ref[0]
            returned.append(dot(up_w[p], grad, ((1,), (1,))))
            mid = projected[p * ranks:(p + 1) * ranks].astype(BF16)
            ups.append(dot(mid, grad, ((1,), (0,))))
        downs = dot(jnp.concatenate(returned, axis=0).astype(BF16), tok[0], ((1,), (0,)))
        return downs, jnp.concatenate(ups, axis=0)

    scatter(0, *adapters(((0, gq),)))
    exchange(0)
    for copy in ret_copies:
        copy.wait_recv()
    gk[0, upper, shifted] = (part[0] + ret_in[0].astype(F32)).astype(BF16)
    gv[0, upper, shifted] = (part[1] + ret_in[1].astype(F32)).astype(BF16)
    for copy in stores[1:]:
        copy.start()
    scatter(1, *adapters(((1, gk), (2, gv))))
    gather(0)
    exchange(1)
    collect(0, first_out)
    gather(1)
    collect(1, last_out)
    for copy in stores:
        copy.wait()
    for copy in kv_copies + ret_copies + copies:
        copy.wait_send()


def finish(
    n_plane, gq_in, gk_in, gv_in, first_in, last_in, gq, gk, gv, gd, gu,
    down, up, held, first, last_two, load_sem, sems
):
    loads = [
        pltpu.make_async_copy(src, held.at[i], load_sem.at[i])
        for i, src in enumerate((gq_in, gk_in, gv_in))
    ]
    copies = [
        pltpu.make_async_copy(held.at[i], dst, sems.at[i]) for i, dst in enumerate((gq, gk, gv))
    ]
    sum_loads = [
        pltpu.make_async_copy(first_in, first, load_sem.at[3]),
        pltpu.make_async_copy(last_in, last_two, load_sem.at[4]),
    ]
    for copy in sum_loads + loads:
        copy.start()
    for copy in sum_loads:
        copy.wait()
    projections, ranks, model_width = down.shape
    wd, wu = model_width // n_plane, up.shape[2] // n_plane
    wide = (wd + wu) // 2
    for sums, start, count in ((first, 0, 1), (last_two, 1, projections - 1)):
        n = count * ranks
        for c in range(n_plane):
            both = sums[c].astype(F32)
            for p in range(count):
                top = both[p * ranks:(p + 1) * ranks]
                low = both[n + p * ranks:n + (p + 1) * ranks]
                down[start + p, :, c * wd:c * wd + wide] = top
                down[start + p, :, c * wd + wide:(c + 1) * wd] = low[:, :wd - wide]
                up[start + p, :, c * wu:(c + 1) * wu] = low[:, wd - wide:]
    last = [
        pltpu.make_async_copy(down, gd, sems.at[3]), pltpu.make_async_copy(up, gu, sems.at[4])
    ]
    for copy in last:
        copy.start()
    for load, copy in zip(loads, copies):
        load.wait()
        copy.start()
    for copy in copies + last:
        copy.wait()


def shards(n_seq, n_dp, tokens, query, key, value, gradient, down_w, up_w):
    _, rows, width = query.shape
    half, half_width = rows // 2, width // 2
    projections, ranks, model_width = down_w.shape
    n_plane, n_z = n_dp * PLANE_SEQ, n_seq // PLANE_SEQ
    across = (model_width + width) // n_plane // 2
    first, last_two = (2 * ranks, across), (2 * (projections - 1) * ranks, across)
    dma = pltpu.SemaphoreType.DMA
    anywhere = pl.BlockSpec(memory_space=pl.ANY)
    *grads, first_sums, last_sums = pl.pallas_call(
        functools.partial(kernel, n_seq, n_dp),
        out_shape=[jax.ShapeDtypeStruct(query.shape, BF16)] * 3
        + [jax.ShapeDtypeStruct((n_plane,) + piece, BF16) for piece in (first, last_two)],
        in_specs=[anywhere] * 7,
        out_specs=[anywhere] * 5,
        scratch_shapes=[
            pltpu.VMEM(ref.shape, BF16)
            for ref in (query, query, query, tokens, query, key, value, gradient, down_w, up_w)
        ]
        + [pltpu.VMEM((2, half, half_width), BF16)] * 3
        + [pltpu.VMEM((2, half, half_width), F32)]
        + [
            pltpu.VMEM((n,) + piece, BF16)
            for piece in (first, last_two)
            for n in (n_plane, n_plane, n_z, n_plane)
        ]
        + [dma((7,)), dma((5,))]
        + [dma((8,))] * 4
        + [dma((2, n)) for n in (n_plane, n_plane, n_z, n_z, n_plane, n_plane)],
        compiler_params=pltpu.CompilerParams(
            collective_id=0, has_side_effects=True, vmem_limit_bytes=58 * 1024 * 1024
        ),
    )(tokens, query, key, value, gradient, down_w, up_w)
    return pl.pallas_call(
        functools.partial(finish, n_plane),
        out_shape=[jax.ShapeDtypeStruct(query.shape, BF16)] * 3
        + [jax.ShapeDtypeStruct(down_w.shape, F32), jax.ShapeDtypeStruct(up_w.shape, F32)],
        in_specs=[anywhere] * 5,
        out_specs=[anywhere] * 5,
        scratch_shapes=[
            pltpu.VMEM(down_w.shape, F32), pltpu.VMEM(up_w.shape, F32),
            pltpu.VMEM((3,) + query.shape, BF16),
            pltpu.VMEM((n_plane,) + first, BF16), pltpu.VMEM((n_plane,) + last_two, BF16),
            dma((5,)), dma((5,)),
        ],
        compiler_params=pltpu.CompilerParams(vmem_limit_bytes=58 * 1024 * 1024),
    )(*grads, first_sums, last_sums)


def solution(mesh):
    split = P("dp", "seq", None)
    return jax.shard_map(
        functools.partial(shards, mesh.shape["seq"], mesh.shape["dp"]),
        mesh=mesh,
        in_specs=(split,) * 5 + (P(), P()),
        out_specs=(split,) * 3 + (P(), P()),
        check_vma=False,
    )
```
